32 devices in a mesh: gx: 4 (over z), gy: 4 (over x, core), col: 2 (over y).
Axes of the slice: x: 2, y: 2, z: 4, core: 2. Of those that a mesh axis runs over, the one named last changes fastest.
Arguments:
- rhs: float32 [4, 4, 2, 1280, 512], P('gx', 'gy', 'col'), may hold values from -6 to 6
- stiff: bfloat16 [4, 4, 2, 1280, 2048], P('gx', 'gy', 'col'), may hold values from -0.125 to 0.125
- inv_local: bfloat16 [4, 4, 2, 1280, 2048], P('gx', 'gy', 'col'), may hold values from -0.125 to 0.125
- basis: bfloat16 [4, 4, 2, 1280, 128], P('gx', 'gy', 'col'), may hold values from -0.15625 to 0.15625
- coarse_inv: float32 [4, 2, 128, 128], P('gy', 'col'), may hold values from -0.5 to 0.5
- colors: int32 [4, 4, 2], P('gx', 'gy', 'col'), may hold values from 0 to 3
- lend: int32 [4, 4, 2, 6], P('gx', 'gy', 'col'), may hold values from 0 to 9
Outputs:
- correction: float32 [4, 4, 2, 1280, 512], P('gx', 'gy', 'col')
The draws below stay inside these ranges and needn't reach their ends.
All inputs are finite; a program needn't handle non-finite values.
Results may differ from the reference program's by a relative error of at most 0.02.
Values may be sent and summed in bfloat16 or wider, within the bound.
A program may use at most 128 MiB of HBM per device.

```python
import jax
import jax.numpy as jnp
from jax import lax

SUB = 2048
BLK = 128
NCOLOR = 4
RHS = 512
OWN = 1280
NCG = 128
N_GX = 4
N_GY = 4
N_COL = 2


def with_ends(values, key, smallest, largest):
    index_at = [jax.random.randint(jax.random.fold_in(key, axis), (), 0, length) for axis, length in enumerate(values.shape)]
    widest = values.shape.index(max(values.shape))
    neighbour = index_at[:widest] + [(index_at[widest] + 1) % values.shape[widest]] + index_at[widest + 1:]
    return values.at[tuple(index_at)].set(smallest).at[tuple(neighbour)].set(largest)


def shard_levels(own_key, dims, cuts, low, high):
    def one(axis_at, blocks):
        steps = jax.random.uniform(jax.random.fold_in(jax.random.fold_in(own_key, 6), axis_at), (blocks,), jnp.float32, low / len(cuts), high / len(cuts))
        return jnp.repeat(jnp.exp(steps), dims[axis_at] // blocks).reshape((-1,) + (1,) * (len(dims) - axis_at - 1))

    gain = one(*cuts[0])
    for cut in cuts[1:]:
        gain = gain * one(*cut)
    return gain


def normal_values(own_key, shape, spread, reach, split=(), kind=jnp.bfloat16):
    array = spread * jax.random.normal(own_key, shape, jnp.float32)
    if split:
        array = array * shard_levels(own_key, shape, split, -0.22, 0.18)
    return jnp.clip(array, -reach, reach).astype(kind)


def setup_inputs(seed: int = 0) -> dict:
    key_of = jax.random.split(jax.random.key(seed), 8)
    rhs = normal_values(key_of[0], (N_GX, N_GY, N_COL, OWN, RHS), 1.0, 6.0, ((0, 4), (1, 4), (2, 2)), jnp.float32)
    stiff = normal_values(key_of[1], (N_GX, N_GY, N_COL, OWN, SUB), SUB ** -0.5, 0.125, ((0, 4), (1, 4), (2, 2)))
    inv_local = normal_values(key_of[2], (N_GX, N_GY, N_COL, OWN, SUB), SUB ** -0.5, 0.125, ((0, 4), (1, 4), (2, 2)))
    basis = normal_values(key_of[3], (N_GX, N_GY, N_COL, OWN, NCG), OWN ** -0.5, 0.15625, ((0, 4), (1, 4), (2, 2)))
    coarse_inv = normal_values(key_of[4], (N_GY, N_COL, NCG, NCG), NCG ** -0.5, 0.5, ((0, 4), (1, 2)), jnp.float32)
    colors = with_ends(jax.random.randint(key_of[5], (N_GX, N_GY, N_COL), 0, NCOLOR), jax.random.fold_in(key_of[5], 1), 0, NCOLOR - 1).astype(jnp.int32)
    lend = with_ends(jax.random.randint(key_of[6], (N_GX, N_GY, N_COL, 6), 0, (SUB - 6 * BLK) // BLK), jax.random.fold_in(key_of[6], 1), 0, ((SUB - 6 * BLK) // BLK) - 1).astype(jnp.int32)
    return {"rhs": rhs, "stiff": stiff, "inv_local": inv_local, "basis": basis, "coarse_inv": coarse_inv, "colors": colors, "lend": lend}


def lower_shift(field, axis):
    size = field.shape[axis]
    zero = jnp.zeros_like(lax.slice_in_dim(field, 0, 1, axis=axis))
    return jnp.concatenate([zero, lax.slice_in_dim(field, 0, size - 1, axis=axis)], axis=axis)


def upper_shift(field, axis):
    size = field.shape[axis]
    zero = jnp.zeros_like(lax.slice_in_dim(field, 0, 1, axis=axis))
    return jnp.concatenate([lax.slice_in_dim(field, 1, size, axis=axis), zero], axis=axis)


def extend(field, lend):
    blocks_own = OWN // BLK
    shaped = field.astype(jnp.float32).reshape(N_GX, N_GY, N_COL, blocks_own, BLK, field.shape[-1])
    onehot = (lend[..., :, None] == jnp.arange(blocks_own, dtype=jnp.int32)).astype(jnp.float32)
    lent = jnp.einsum("abckn,abcnir->abckir", onehot, shaped)
    pieces = [field.astype(jnp.float32)]
    for axis_num in range(3):
        pieces.append(lower_shift(lent[:, :, :, 2 * axis_num + 1], axis_num))
        pieces.append(upper_shift(lent[:, :, :, 2 * axis_num], axis_num))
    return jnp.concatenate(pieces, axis=3).astype(jnp.bfloat16)


def apply_rows(matrix, local):
    count = N_GX * N_GY * N_COL
    flat_m = matrix.reshape(count, matrix.shape[-2], matrix.shape[-1])
    flat_v = local.reshape(count, local.shape[-2], local.shape[-1])

    def one(pair):
        return jnp.dot(pair[0].astype(jnp.float32), pair[1].astype(jnp.float32), preferred_element_type=jnp.float32)

    out = lax.map(one, (flat_m, flat_v))
    return out.reshape(N_GX, N_GY, N_COL, matrix.shape[-2], local.shape[-1])


def solve_color(inv_local, local, colors, color_now):
    count = N_GX * N_GY * N_COL
    flat_m = inv_local.reshape(count, OWN, SUB)
    flat_v = local.reshape(count, SUB, local.shape[-1])
    flat_c = colors.reshape(count)

    def one(triple):
        matrix, vector, color = triple
        return lax.cond(color == color_now,
                        lambda: jnp.dot(matrix.astype(jnp.float32), vector.astype(jnp.float32), preferred_element_type=jnp.float32).astype(jnp.bfloat16),
                        lambda: jnp.zeros((OWN, vector.shape[-1]), jnp.bfloat16))

    out = lax.map(one, (flat_m, flat_v, flat_c))
    return out.reshape(N_GX, N_GY, N_COL, OWN, local.shape[-1])


def reference(rhs, stiff, inv_local, basis, coarse_inv, colors, lend):
    resid_b = rhs.astype(jnp.bfloat16)
    basis_f = basis.astype(jnp.float32)
    partial_value = jnp.einsum("abcon,abcor->abcnr", basis_f, resid_b.astype(jnp.float32))
    coarse_rhs = jnp.sum(partial_value, axis=0)
    coarse_sol = jnp.einsum("bcmn,bcnr->bcmr", coarse_inv, coarse_rhs, precision=lax.Precision.HIGHEST).astype(jnp.bfloat16)
    coarse_delta = jnp.einsum("abcon,bcnr->abcor", basis_f, coarse_sol.astype(jnp.float32)).astype(jnp.bfloat16)
    acc = coarse_delta.astype(jnp.float32)
    resid = rhs - apply_rows(stiff, extend(coarse_delta, lend))
    for color_now in range(NCOLOR):
        local_b = extend(resid.astype(jnp.bfloat16), lend)
        delta = solve_color(inv_local, local_b, colors, color_now)
        acc = acc + delta.astype(jnp.float32)
        if color_now < NCOLOR - 1:
            resid = resid - apply_rows(stiff, extend(delta, lend))
    return acc
```

```python
import functools

import jax
import jax.numpy as jnp
from jax import lax
from jax.experimental import pallas as pl
from jax.experimental.pallas import tpu as pltpu
from jax.sharding import PartitionSpec as P

BLK = 128
NCOLOR = 4
TM = 256
HALVES = 2
MESH = pl.DeviceIdType.MESH
BF = jnp.bfloat16
F32 = jnp.float32
AXES = ("gx", "gx", "gy", "gy", "col", "col")


def flat(x):
    return x.reshape(-1, x.shape[-1])


def dot(a, b):
    return jnp.dot(a, b, preferred_element_type=F32)


def kernel(sizes, colors, lend, rhs, stiff, inv, basis, emat, out,
           kmat, ainv, phi, ecoarse, resid, resid_b, y, delta, acc, out_b,
           margin, lent, k_lent, e_lent, weights, sols, base_m, base_l,
           part, line_in, line_out,
           load_sem, store_sem, send_sem, recv_sem, sol_send, sol_recv,
           base_send, base_recv, line_send, line_recv):
    own = ainv.shape[0]
    ncg = phi.shape[2]
    width = resid.shape[3]
    at = {axis: lax.axis_index(axis) for axis in sizes}

    def has(side):
        i = at[AXES[side]]
        return i > 0 if side % 2 == 0 else i < sizes[AXES[side]] - 1

    def peer(side):
        i = at[AXES[side]]
        return {AXES[side]: i - 1 if side % 2 == 0 else i + 1}

    loads = [pltpu.make_async_copy(basis.at[0, 0, 0], phi, load_sem.at[0])]
    for h in range(HALVES):
        loads.append(pltpu.make_async_copy(
            rhs.at[0, 0, 0, :, :, h * width:(h + 1) * width], resid.at[h], load_sem.at[1 + h]))
    loads.append(pltpu.make_async_copy(emat.at[0, 0], ecoarse, load_sem.at[3]))
    loads.append(pltpu.make_async_copy(stiff.at[0, 0, 0], kmat, load_sem.at[4]))
    loads.append(pltpu.make_async_copy(inv.at[0, 0, 0], ainv, load_sem.at[5]))
    for load in loads:
        load.start()

    barrier = pltpu.get_barrier_semaphore()
    for side in range(6):
        @pl.when(has(side))
        def _(side=side):
            pl.semaphore_signal(barrier, inc=1, device_id=peer(side), device_id_type=MESH)

    for side in range(6):
        @pl.when(jnp.logical_not(has(side)))
        def _(side=side):
            rows = pl.ds(side * BLK, BLK)
            base_m[rows, :] = jnp.zeros((BLK, ncg), BF)
            for r in range(2 * NCOLOR - 1):
                for h in range(HALVES):
                    margin[r, h, rows, :] = jnp.zeros((BLK, width), BF)
            if side >= 2:
                for h in range(HALVES):
                    sols[h, pl.ds((side - 1) * ncg, ncg), :] = jnp.zeros((ncg, width), BF)
            else:
                for h in range(HALVES):
                    line_in[side, h] = jnp.zeros((ncg, width), BF)

    picks = [lend[0, 0, 0, side] for side in range(6)]
    color = colors[0, 0, 0]

    pl.semaphore_wait(barrier, sum(has(side).astype(jnp.int32) for side in range(6)))

    def margin_copy(r, h, side):
        return pltpu.make_async_remote_copy(
            src_ref=lent.at[r, h, pl.ds(side * BLK, BLK)],
            dst_ref=margin.at[r, h, pl.ds((side ^ 1) * BLK, BLK)],
            send_sem=send_sem.at[r, h, side], recv_sem=recv_sem.at[r, h, side ^ 1],
            device_id=peer(side), device_id_type=MESH)

    def margin_arrival(r, h, side):
        return pltpu.make_async_remote_copy(
            src_ref=lent.at[r, h, pl.ds(side * BLK, BLK)],
            dst_ref=margin.at[r, h, pl.ds(side * BLK, BLK)],
            send_sem=send_sem.at[r, h, side], recv_sem=recv_sem.at[r, h, side],
            device_id=peer(side), device_id_type=MESH)

    def base_copy(side, slot):
        return pltpu.make_async_remote_copy(
            src_ref=base_l.at[pl.ds(side * BLK, BLK)],
            dst_ref=base_m.at[pl.ds(slot * BLK, BLK)],
            send_sem=base_send.at[side], recv_sem=base_recv.at[slot],
            device_id=peer(side), device_id_type=MESH)

    def sol_copy(h, side, slot):
        return pltpu.make_async_remote_copy(
            src_ref=sols.at[h, pl.ds(0, ncg)],
            dst_ref=sols.at[h, pl.ds((slot - 1) * ncg, ncg)],
            send_sem=sol_send.at[h, side], recv_sem=sol_recv.at[h, slot],
            device_id=peer(side), device_id_type=MESH)

    def line_copy(h, side, slot):
        return pltpu.make_async_remote_copy(
            src_ref=line_out.at[side, h], dst_ref=line_in.at[slot, h],
            send_sem=line_send.at[side, h], recv_sem=line_recv.at[slot, h],
            device_id=peer(side), device_id_type=MESH)

    def each(sides, make, action):
        for side in sides:
            @pl.when(has(side))
            def _(side=side):
                getattr(make(side), action)()

    def send_margins(r, h):
        each(range(6), functools.partial(margin_copy, r, h), "start")

    def await_margins(r, h):
        each(range(6), functools.partial(margin_arrival, r, h), "wait_recv")

    def tiles(body, rows=own):
        def step(i, carry):
            body(pl.ds(pl.multiple_of(i * TM, TM), TM), pl.ds(i * (TM // BLK), TM // BLK))
            return carry
        lax.fori_loop(0, rows // TM, step, 0)

    loads[0].wait()
    for side in range(6):
        base_l[pl.ds(side * BLK, BLK), :] = phi[picks[side]]
    each(range(6), lambda side: base_copy(side, side ^ 1), "start")
    phi_t = phi[...].reshape(own, ncg).T
    for h in range(HALVES):
        loads[1 + h].wait()
        part[h] = dot(phi_t, resid[h].reshape(own, width).astype(BF))

    n_line = sizes["gx"]
    low = at["gx"] < n_line // 2

    def pass_on(h, slot):
        @pl.when(has(slot))
        def _():
            line_copy(h, slot, slot).wait_recv()

        @pl.when(has(slot ^ 1))
        def _():
            line_out[slot ^ 1, h] = (line_in[slot, h].astype(F32) + part[h]).astype(BF)
            line_copy(h, slot ^ 1, slot).start()

    def pass_all(slot):
        for h in range(HALVES):
            pass_on(h, slot)

    pl.when(low)(lambda: pass_all(0))
    pl.when(jnp.logical_not(low))(lambda: pass_all(1))

    loads[4].wait()
    for side in range(6):
        k_lent[pl.ds(side * BLK, BLK), :] = kmat[picks[side], :, 0:own]
    each(range(6), lambda side: base_copy(side, side), "wait_recv")

    def weigh(rows, blocks):
        first = dot(flat(kmat[blocks, :, 0:own]), phi[...].reshape(own, ncg))
        first = first + dot(flat(kmat[blocks, :, own:own + 2 * BLK]), base_m[0:2 * BLK, :])
        weights[rows, 0:ncg] = first.astype(BF)
        for side in range(2, 6):
            weights[rows, (side - 1) * ncg:side * ncg] = dot(
                flat(kmat[blocks, :, own + side * BLK:own + (side + 1) * BLK]),
                base_m[side * BLK:(side + 1) * BLK, :]).astype(BF)

    tiles(weigh)

    pl.when(low)(lambda: pass_all(1))
    pl.when(jnp.logical_not(low))(lambda: pass_all(0))

    loads[3].wait()
    for h in range(HALVES):
        total = line_in[0, h].astype(F32) + part[h] + line_in[1, h].astype(F32)
        sols[h, 0:ncg, :] = jnp.dot(
            ecoarse[...], total, precision=lax.Precision.HIGHEST,
            preferred_element_type=F32).astype(BF)
        each(range(2, 6), lambda side, h=h: sol_copy(h, side, side ^ 1), "start")
    for h in range(HALVES):
        def coarse(rows, blocks, h=h):
            acc[h, rows, :] = dot(flat(phi[blocks]), sols[h, 0:ncg, :])
        tiles(coarse)

    def lend_resid(r, h, with_own):
        for side in range(6):
            block = pl.ds(side * BLK, BLK)
            value = resid[h, picks[side]]
            if with_own:
                value = value - e_lent[h, block, :]
            lent[r, h, block, :] = value.astype(BF)
        send_margins(r, h)

    for h in range(HALVES):
        each(range(2, 6), lambda side, h=h: sol_copy(h, side, side), "wait_recv")

        def first_resid(rows, blocks, h=h):
            value = flat(resid[h, blocks]) - dot(weights[rows, :], sols[h])
            resid[h, blocks] = value.reshape(-1, BLK, width)
            resid_b[h, rows, :] = value.astype(BF)
        tiles(first_resid)
        lend_resid(0, h, False)

    loads[5].wait()

    def solve_own(h):
        def body(rows, blocks):
            y[h, rows, :] = dot(ainv[rows, 0:own], resid_b[h])
        tiles(body)

    for h in range(HALVES):
        solve_own(h)

    for c in range(NCOLOR):
        mine = (color == c).astype(F32)
        last = c == NCOLOR - 1
        for h in range(HALVES):
            await_margins(2 * c, h)

            def solve(rows, blocks, h=h):
                value = (y[h, rows, :] + dot(ainv[rows, own:], margin[2 * c, h])) * mine
                if last:
                    out_b[h, rows, :] = (acc[h, rows, :] + value).astype(BF)
                else:
                    delta[h, blocks] = value.astype(BF).reshape(-1, BLK, width)
                    acc[h, rows, :] += value
            tiles(solve)
            if last:
                pltpu.make_async_copy(
                    out_b.at[h], out.at[0, 0, 0, :, h * width:(h + 1) * width],
                    store_sem.at[h]).start()
            else:
                for side in range(6):
                    lent[2 * c + 1, h, pl.ds(side * BLK, BLK), :] = delta[h, picks[side]]
                send_margins(2 * c + 1, h)
        if last:
            break
        for h in range(HALVES):
            def own_part(rows, blocks, h=h):
                value = dot(k_lent[rows, :], delta[h].reshape(own, width))
                if c == 0:
                    e_lent[h, rows, :] = value
                else:
                    e_lent[h, rows, :] += value
            tiles(own_part, 6 * BLK)
        for h in range(HALVES):
            await_margins(2 * c + 1, h)

            def update(rows, blocks, h=h):
                value = flat(resid[h, blocks]) - dot(flat(kmat[blocks, :, own:]), margin[2 * c + 1, h])
                resid[h, blocks] = value.reshape(-1, BLK, width)
                resid_b[h, rows, :] = value.astype(BF)
            tiles(update)
            lend_resid(2 * c + 2, h, True)
        for h in range(HALVES):
            solve_own(h)

    for h in range(HALVES):
        pltpu.make_async_copy(
            out_b.at[h], out.at[0, 0, 0, :, h * width:(h + 1) * width], store_sem.at[h]).wait()
    each(range(6), lambda side: base_copy(side, side ^ 1), "wait_send")
    for h in range(HALVES):
        each(range(2), lambda side, h=h: line_copy(h, side, side ^ 1), "wait_send")
        each(range(2, 6), lambda side, h=h: sol_copy(h, side, side ^ 1), "wait_send")
        for r in range(2 * NCOLOR - 1):
            each(range(6), functools.partial(margin_copy, r, h), "wait_send")


def in_blocks(x):
    return x.reshape(x.shape[:-2] + (x.shape[-2] // BLK, BLK, x.shape[-1]))


def body(sizes, rhs, stiff, inv_local, basis, coarse_inv, colors, lend):
    own, nrhs = rhs.shape[-2:]
    sub = stiff.shape[-1]
    ncg = basis.shape[-1]
    width = nrhs // HALVES
    count = own // BLK
    rounds = 2 * NCOLOR - 1
    edge = 6 * BLK
    dma = pltpu.SemaphoreType.DMA
    smem = pl.BlockSpec(memory_space=pltpu.SMEM)
    anyw = pl.BlockSpec(memory_space=pl.ANY)
    result = pl.pallas_call(
        functools.partial(kernel, sizes),
        out_shape=jax.ShapeDtypeStruct(rhs.shape, BF),
        in_specs=[smem, smem] + [anyw] * 5,
        out_specs=anyw,
        scratch_shapes=[
            pltpu.VMEM((count, BLK, sub), BF),
            pltpu.VMEM((own, sub), BF),
            pltpu.VMEM((count, BLK, ncg), BF),
            pltpu.VMEM((ncg, ncg), F32),
            pltpu.VMEM((HALVES, count, BLK, width), F32),
            pltpu.VMEM((HALVES, own, width), BF),
            pltpu.VMEM((HALVES, own, width), F32),
            pltpu.VMEM((HALVES, count, BLK, width), BF),
            pltpu.VMEM((HALVES, own, width), F32),
            pltpu.VMEM((HALVES, own, width), BF),
            pltpu.VMEM((rounds, HALVES, edge, width), BF),
            pltpu.VMEM((rounds, HALVES, edge, width), BF),
            pltpu.VMEM((edge, own), BF),
            pltpu.VMEM((HALVES, edge, width), F32),
            pltpu.VMEM((own, 5 * ncg), BF),
            pltpu.VMEM((HALVES, 5 * ncg, width), BF),
            pltpu.VMEM((edge, ncg), BF),
            pltpu.VMEM((edge, ncg), BF),
            pltpu.VMEM((HALVES, ncg, width), F32),
            pltpu.VMEM((2, HALVES, ncg, width), BF),
            pltpu.VMEM((2, HALVES, ncg, width), BF),
            dma((6,)),
            dma((HALVES,)),
            dma((rounds, HALVES, 6)),
            dma((rounds, HALVES, 6)),
            dma((HALVES, 6)),
            dma((HALVES, 6)),
            dma((6,)),
            dma((6,)),
            dma((2, HALVES)),
            dma((2, HALVES)),
        ],
        compiler_params=pltpu.CompilerParams(
            collective_id=0, has_side_effects=True, vmem_limit_bytes=58 * 2**20),
    )(colors, lend, in_blocks(rhs), in_blocks(stiff), inv_local, in_blocks(basis), coarse_inv)
    return result.astype(F32)


def solution(mesh):
    in_specs = (
        P("gx", "gy", "col", None, None),
        P("gx", "gy", "col", None, None),
        P("gx", "gy", "col", None, None),
        P("gx", "gy", "col", None, None),
        P("gy", "col", None, None),
        P("gx", "gy", "col"),
        P("gx", "gy", "col", None),
    )
    out_specs = P("gx", "gy", "col", None, None)
    return jax.shard_map(functools.partial(body, dict(mesh.shape)), mesh=mesh,
                         in_specs=in_specs, out_specs=out_specs, check_vma=False)
```

```python
import functools

import jax
import jax.numpy as jnp
from jax import lax
from jax.experimental import pallas as pl
from jax.experimental.pallas import tpu as pltpu
from jax.sharding import PartitionSpec as P

BLK = 128
NCOLOR = 4
TM = 640
TE = 768
HALVES = 2
MESH = pl.DeviceIdType.MESH
BF = jnp.bfloat16
F32 = jnp.float32
AXES = ("gx", "gx", "gy", "gy", "col", "col")


def flat(x):
    return x.reshape(-1, x.shape[-1])


def dot(a, b):
    return jnp.dot(a, b, preferred_element_type=F32)


def kernel(sizes, colors, lend, rhs, stiff, inv, basis, emat, out,
           kmat, ainv, phi, ecoarse, resid, resid_b, y, delta, acc, out_b,
           margin, lent, k_lent, e_lent, weights, sols, base_m, base_l,
           part, line_in, line_out,
           load_sem, store_sem, send_sem, recv_sem, sol_send, sol_recv,
           base_send, base_recv, line_send, line_recv):
    own = ainv.shape[0]
    ncg = phi.shape[2]
    width = resid.shape[3]
    at = {axis: lax.axis_index(axis) for axis in sizes}

    def has(side):
        i = at[AXES[side]]
        return i > 0 if side % 2 == 0 else i < sizes[AXES[side]] - 1

    def peer(side):
        i = at[AXES[side]]
        return {AXES[side]: i - 1 if side % 2 == 0 else i + 1}

    loads = [pltpu.make_async_copy(basis.at[0, 0, 0], phi, load_sem.at[0])]
    for h in range(HALVES):
        loads.append(pltpu.make_async_copy(
            rhs.at[0, 0, 0, :, :, h * width:(h + 1) * width], resid.at[h], load_sem.at[1 + h]))
    loads.append(pltpu.make_async_copy(emat.at[0, 0], ecoarse, load_sem.at[3]))
    loads.append(pltpu.make_async_copy(stiff.at[0, 0, 0], kmat, load_sem.at[4]))
    loads.append(pltpu.make_async_copy(inv.at[0, 0, 0], ainv, load_sem.at[5]))
    for load in loads:
        load.start()

    barrier = pltpu.get_barrier_semaphore()
    for side in range(6):
        @pl.when(has(side))
        def _(side=side):
            pl.semaphore_signal(barrier, inc=1, device_id=peer(side), device_id_type=MESH)

    for side in range(6):
        @pl.when(jnp.logical_not(has(side)))
        def _(side=side):
            rows = pl.ds(side * BLK, BLK)
            base_m[rows, :] = jnp.zeros((BLK, ncg), BF)
            for r in range(2 * NCOLOR - 1):
                for h in range(HALVES):
                    margin[r, h, rows, :] = jnp.zeros((BLK, width), BF)
            if side >= 2:
                for h in range(HALVES):
                    sols[h, pl.ds((side - 1) * ncg, ncg), :] = jnp.zeros((ncg, width), BF)
            else:
                for h in range(HALVES):
                    line_in[side, h] = jnp.zeros((ncg, width), BF)

    picks = [lend[0, 0, 0, side] for side in range(6)]
    color = colors[0, 0, 0]

    pl.semaphore_wait(barrier, sum(has(side).astype(jnp.int32) for side in range(6)))

    def margin_copy(r, h, side):
        return pltpu.make_async_remote_copy(
            src_ref=lent.at[r, h, pl.ds(side * BLK, BLK)],
            dst_ref=margin.at[r, h, pl.ds((side ^ 1) * BLK, BLK)],
            send_sem=send_sem.at[r, h, side], recv_sem=recv_sem.at[r, h, side ^ 1],
            device_id=peer(side), device_id_type=MESH)

    def margin_arrival(r, h, side):
        return pltpu.make_async_remote_copy(
            src_ref=lent.at[r, h, pl.ds(side * BLK, BLK)],
            dst_ref=margin.at[r, h, pl.ds(side * BLK, BLK)],
            send_sem=send_sem.at[r, h, side], recv_sem=recv_sem.at[r, h, side],
            device_id=peer(side), device_id_type=MESH)

    def base_copy(side, slot):
        return pltpu.make_async_remote_copy(
            src_ref=base_l.at[pl.ds(side * BLK, BLK)],
            dst_ref=base_m.at[pl.ds(slot * BLK, BLK)],
            send_sem=base_send.at[side], recv_sem=base_recv.at[slot],
            device_id=peer(side), device_id_type=MESH)

    def sol_copy(h, side, slot):
        return pltpu.make_async_remote_copy(
            src_ref=sols.at[h, pl.ds(0, ncg)],
            dst_ref=sols.at[h, pl.ds((slot - 1) * ncg, ncg)],
            send_sem=sol_send.at[h, side], recv_sem=sol_recv.at[h, slot],
            device_id=peer(side), device_id_type=MESH)

    def line_copy(h, side, slot):
        return pltpu.make_async_remote_copy(
            src_ref=line_out.at[side, h], dst_ref=line_in.at[slot, h],
            send_sem=line_send.at[side, h], recv_sem=line_recv.at[slot, h],
            device_id=peer(side), device_id_type=MESH)

    def each(sides, make, action):
        for side in sides:
            @pl.when(has(side))
            def _(side=side):
                getattr(make(side), action)()

    def send_margins(r, h):
        each(range(6), functools.partial(margin_copy, r, h), "start")

    def await_margins(r, h):
        each(range(6), functools.partial(margin_arrival, r, h), "wait_recv")

    def tiles(body, rows=own):
        tm = TM if rows == own else TE

        def step(i, carry):
            body(pl.ds(pl.multiple_of(i * tm, tm), tm), pl.ds(i * (tm // BLK), tm // BLK))
            return carry
        lax.fori_loop(0, rows // tm, step, 0)

    loads[0].wait()
    for side in range(6):
        base_l[pl.ds(side * BLK, BLK), :] = phi[picks[side]]
    each(range(6), lambda side: base_copy(side, side ^ 1), "start")
    phi_t = phi[...].reshape(own, ncg).T
    for h in range(HALVES):
        loads[1 + h].wait()
        part[h] = dot(phi_t, resid[h].reshape(own, width).astype(BF))

    n_line = sizes["gx"]
    low = at["gx"] < n_line // 2

    def pass_on(h, slot):
        @pl.when(has(slot))
        def _():
            line_copy(h, slot, slot).wait_recv()

        @pl.when(has(slot ^ 1))
        def _():
            line_out[slot ^ 1, h] = (line_in[slot, h].astype(F32) + part[h]).astype(BF)
            line_copy(h, slot ^ 1, slot).start()

    def pass_all(slot):
        for h in range(HALVES):
            pass_on(h, slot)

    pl.when(low)(lambda: pass_all(0))
    pl.when(jnp.logical_not(low))(lambda: pass_all(1))

    loads[4].wait()
    for side in range(6):
        k_lent[pl.ds(side * BLK, BLK), :] = kmat[picks[side], :, 0:own]
    each(range(6), lambda side: base_copy(side, side), "wait_recv")

    def weigh(rows, blocks):
        first = dot(flat(kmat[blocks, :, 0:own]), phi[...].reshape(own, ncg))
        first = first + dot(flat(kmat[blocks, :, own:own + 2 * BLK]), base_m[0:2 * BLK, :])
        weights[rows, 0:ncg] = first.astype(BF)
        for side in range(2, 6):
            weights[rows, (side - 1) * ncg:side * ncg] = dot(
                flat(kmat[blocks, :, own + side * BLK:own + (side + 1) * BLK]),
                base_m[side * BLK:(side + 1) * BLK, :]).astype(BF)

    tiles(weigh)

    pl.when(low)(lambda: pass_all(1))
    pl.when(jnp.logical_not(low))(lambda: pass_all(0))

    loads[3].wait()
    for h in range(HALVES):
        total = line_in[0, h].astype(F32) + part[h] + line_in[1, h].astype(F32)
        sols[h, 0:ncg, :] = jnp.dot(
            ecoarse[...], total, precision=lax.Precision.HIGHEST,
            preferred_element_type=F32).astype(BF)
        each(range(2, 6), lambda side, h=h: sol_copy(h, side, side ^ 1), "start")
    for h in range(HALVES):
        def coarse(rows, blocks, h=h):
            acc[h, rows, :] = dot(flat(phi[blocks]), sols[h, 0:ncg, :])
        tiles(coarse)

    def lend_resid(r, h, with_own):
        for side in range(6):
            block = pl.ds(side * BLK, BLK)
            value = resid[h, picks[side]]
            if with_own:
                value = value - e_lent[h, block, :]
            lent[r, h, block, :] = value.astype(BF)
        send_margins(r, h)

    for h in range(HALVES):
        each(range(2, 6), lambda side, h=h: sol_copy(h, side, side), "wait_recv")

        def first_resid(rows, blocks, h=h):
            value = flat(resid[h, blocks]) - dot(weights[rows, :], sols[h])
            resid[h, blocks] = value.reshape(-1, BLK, width)
            resid_b[h, rows, :] = value.astype(BF)
        tiles(first_resid)
        lend_resid(0, h, False)

    loads[5].wait()

    def solve_own(h):
        def body(rows, blocks):
            y[h, rows, :] = dot(ainv[rows, 0:own], resid_b[h])
        tiles(body)

    for h in range(HALVES):
        solve_own(h)

    for c in range(NCOLOR):
        mine = (color == c).astype(F32)
        last = c == NCOLOR - 1
        for h in range(HALVES):
            await_margins(2 * c, h)

            def solve(rows, blocks, h=h):
                value = (y[h, rows, :] + dot(ainv[rows, own:], margin[2 * c, h])) * mine
                if last:
                    out_b[h, rows, :] = (acc[h, rows, :] + value).astype(BF)
                else:
                    delta[h, blocks] = value.astype(BF).reshape(-1, BLK, width)
                    acc[h, rows, :] += value
            tiles(solve)
            if last:
                pltpu.make_async_copy(
                    out_b.at[h], out.at[0, 0, 0, :, h * width:(h + 1) * width],
                    store_sem.at[h]).start()
            else:
                for side in range(6):
                    lent[2 * c + 1, h, pl.ds(side * BLK, BLK), :] = delta[h, picks[side]]
                send_margins(2 * c + 1, h)
        if last:
            break
        for h in range(HALVES):
            def own_part(rows, blocks, h=h):
                value = dot(k_lent[rows, :], delta[h].reshape(own, width))
                if c == 0:
                    e_lent[h, rows, :] = value
                else:
                    e_lent[h, rows, :] += value
            tiles(own_part, 6 * BLK)
        for h in range(HALVES):
            await_margins(2 * c + 1, h)

            def update(rows, blocks, h=h):
                value = flat(resid[h, blocks]) - dot(flat(kmat[blocks, :, own:]), margin[2 * c + 1, h])
                resid[h, blocks] = value.reshape(-1, BLK, width)
                resid_b[h, rows, :] = value.astype(BF)
            tiles(update)
            lend_resid(2 * c + 2, h, True)
        for h in range(HALVES):
            solve_own(h)

    for h in range(HALVES):
        pltpu.make_async_copy(
            out_b.at[h], out.at[0, 0, 0, :, h * width:(h + 1) * width], store_sem.at[h]).wait()
    each(range(6), lambda side: base_copy(side, side ^ 1), "wait_send")
    for h in range(HALVES):
        each(range(2), lambda side, h=h: line_copy(h, side, side ^ 1), "wait_send")
        each(range(2, 6), lambda side, h=h: sol_copy(h, side, side ^ 1), "wait_send")
        for r in range(2 * NCOLOR - 1):
            each(range(6), functools.partial(margin_copy, r, h), "wait_send")


def in_blocks(x):
    return x.reshape(x.shape[:-2] + (x.shape[-2] // BLK, BLK, x.shape[-1]))


def body(sizes, rhs, stiff, inv_local, basis, coarse_inv, colors, lend):
    own, nrhs = rhs.shape[-2:]
    sub = stiff.shape[-1]
    ncg = basis.shape[-1]
    width = nrhs // HALVES
    count = own // BLK
    rounds = 2 * NCOLOR - 1
    edge = 6 * BLK
    dma = pltpu.SemaphoreType.DMA
    smem = pl.BlockSpec(memory_space=pltpu.SMEM)
    anyw = pl.BlockSpec(memory_space=pl.ANY)
    result = pl.pallas_call(
        functools.partial(kernel, sizes),
        out_shape=jax.ShapeDtypeStruct(rhs.shape, BF),
        in_specs=[smem, smem] + [anyw] * 5,
        out_specs=anyw,
        scratch_shapes=[
            pltpu.VMEM((count, BLK, sub), BF),
            pltpu.VMEM((own, sub), BF),
            pltpu.VMEM((count, BLK, ncg), BF),
            pltpu.VMEM((ncg, ncg), F32),
            pltpu.VMEM((HALVES, count, BLK, width), F32),
            pltpu.VMEM((HALVES, own, width), BF),
            pltpu.VMEM((HALVES, own, width), F32),
            pltpu.VMEM((HALVES, count, BLK, width), BF),
            pltpu.VMEM((HALVES, own, width), F32),
            pltpu.VMEM((HALVES, own, width), BF),
            pltpu.VMEM((rounds, HALVES, edge, width), BF),
            pltpu.VMEM((rounds, HALVES, edge, width), BF),
            pltpu.VMEM((edge, own), BF),
            pltpu.VMEM((HALVES, edge, width), F32),
            pltpu.VMEM((own, 5 * ncg), BF),
            pltpu.VMEM((HALVES, 5 * ncg, width), BF),
            pltpu.VMEM((edge, ncg), BF),
            pltpu.VMEM((edge, ncg), BF),
            pltpu.VMEM((HALVES, ncg, width), F32),
            pltpu.VMEM((2, HALVES, ncg, width), BF),
            pltpu.VMEM((2, HALVES, ncg, width), BF),
            dma((6,)),
            dma((HALVES,)),
            dma((rounds, HALVES, 6)),
            dma((rounds, HALVES, 6)),
            dma((HALVES, 6)),
            dma((HALVES, 6)),
            dma((6,)),
            dma((6,)),
            dma((2, HALVES)),
            dma((2, HALVES)),
        ],
        compiler_params=pltpu.CompilerParams(
            collective_id=0, has_side_effects=True, vmem_limit_bytes=58 * 2**20),
    )(colors, lend, in_blocks(rhs), in_blocks(stiff), inv_local, in_blocks(basis), coarse_inv)
    return result.astype(F32)


def solution(mesh):
    in_specs = (
        P("gx", "gy", "col", None, None),
        P("gx", "gy", "col", None, None),
        P("gx", "gy", "col", None, None),
        P("gx", "gy", "col", None, None),
        P("gy", "col", None, None),
        P("gx", "gy", "col"),
        P("gx", "gy", "col", None),
    )
    out_specs = P("gx", "gy", "col", None, None)
    return jax.shard_map(functools.partial(body, dict(mesh.shape)), mesh=mesh,
                         in_specs=in_specs, out_specs=out_specs, check_vma=False)
```

```python
import functools

import jax
import jax.numpy as jnp
from jax import lax
from jax.experimental import pallas as pl
from jax.experimental.pallas import tpu as pltpu
from jax.sharding import PartitionSpec as P

BLK = 128
NCOLOR = 4
TM = 640
TE = 768
HALVES = 2
MESH = pl.DeviceIdType.MESH
BF = jnp.bfloat16
F32 = jnp.float32
AXES = ("gx", "gx", "gy", "gy", "col", "col")


def flat(x):
    return x.reshape(-1, x.shape[-1])


def dot(a, b):
    return jnp.dot(a, b, preferred_element_type=F32)


def kernel(sizes, colors, lend, rhs, stiff, inv, basis, emat, out,
           kmat, ainv, phi, ecoarse, resid, resid_b, y, delta, acc, out_b,
           margin, lent, k_lent, e_lent, weights, sols, base_m, base_l,
           part, line_in, line_out,
           load_sem, store_sem, send_sem, recv_sem, sol_send, sol_recv,
           base_send, base_recv, line_send, line_recv):
    own = ainv.shape[0]
    ncg = phi.shape[2]
    width = resid.shape[3]
    at = {axis: lax.axis_index(axis) for axis in sizes}

    def has(side):
        i = at[AXES[side]]
        return i > 0 if side % 2 == 0 else i < sizes[AXES[side]] - 1

    def peer(side):
        i = at[AXES[side]]
        return {AXES[side]: i - 1 if side % 2 == 0 else i + 1}

    loads = [pltpu.make_async_copy(basis.at[0, 0, 0], phi, load_sem.at[0])]
    for h in range(HALVES):
        loads.append(pltpu.make_async_copy(
            rhs.at[0, 0, 0, :, :, h * width:(h + 1) * width], resid.at[h], load_sem.at[1 + h]))
    loads.append(pltpu.make_async_copy(emat.at[0, 0], ecoarse, load_sem.at[3]))
    loads.append(pltpu.make_async_copy(stiff.at[0, 0, 0], kmat, load_sem.at[4]))
    loads.append(pltpu.make_async_copy(inv.at[0, 0, 0], ainv, load_sem.at[5]))
    for load in loads[:4]:
        load.start()

    barrier = pltpu.get_barrier_semaphore()
    for side in range(6):
        @pl.when(has(side))
        def _(side=side):
            pl.semaphore_signal(barrier, inc=1, device_id=peer(side), device_id_type=MESH)

    for side in range(6):
        @pl.when(jnp.logical_not(has(side)))
        def _(side=side):
            rows = pl.ds(side * BLK, BLK)
            base_m[rows, :] = jnp.zeros((BLK, ncg), BF)
            for r in range(2 * NCOLOR - 1):
                for h in range(HALVES):
                    margin[r, h, rows, :] = jnp.zeros((BLK, width), BF)
            if side >= 2:
                for h in range(HALVES):
                    sols[h, pl.ds((side - 1) * ncg, ncg), :] = jnp.zeros((ncg, width), BF)
            else:
                for h in range(HALVES):
                    line_in[side, h] = jnp.zeros((ncg, width), BF)

    picks = [lend[0, 0, 0, side] for side in range(6)]
    color = colors[0, 0, 0]

    pl.semaphore_wait(barrier, sum(has(side).astype(jnp.int32) for side in range(6)))

    def margin_copy(r, h, side):
        return pltpu.make_async_remote_copy(
            src_ref=lent.at[r, h, pl.ds(side * BLK, BLK)],
            dst_ref=margin.at[r, h, pl.ds((side ^ 1) * BLK, BLK)],
            send_sem=send_sem.at[r, h, side], recv_sem=recv_sem.at[r, h, side ^ 1],
            device_id=peer(side), device_id_type=MESH)

    def margin_arrival(r, h, side):
        return pltpu.make_async_remote_copy(
            src_ref=lent.at[r, h, pl.ds(side * BLK, BLK)],
            dst_ref=margin.at[r, h, pl.ds(side * BLK, BLK)],
            send_sem=send_sem.at[r, h, side], recv_sem=recv_sem.at[r, h, side],
            device_id=peer(side), device_id_type=MESH)

    def base_copy(side, slot):
        return pltpu.make_async_remote_copy(
            src_ref=base_l.at[pl.ds(side * BLK, BLK)],
            dst_ref=base_m.at[pl.ds(slot * BLK, BLK)],
            send_sem=base_send.at[side], recv_sem=base_recv.at[slot],
            device_id=peer(side), device_id_type=MESH)

    def sol_copy(h, side, slot):
        return pltpu.make_async_remote_copy(
            src_ref=sols.at[h, pl.ds(0, ncg)],
            dst_ref=sols.at[h, pl.ds((slot - 1) * ncg, ncg)],
            send_sem=sol_send.at[h, side], recv_sem=sol_recv.at[h, slot],
            device_id=peer(side), device_id_type=MESH)

    def line_copy(h, side, slot):
        return pltpu.make_async_remote_copy(
            src_ref=line_out.at[side, h], dst_ref=line_in.at[slot, h],
            send_sem=line_send.at[side, h], recv_sem=line_recv.at[slot, h],
            device_id=peer(side), device_id_type=MESH)

    def each(sides, make, action):
        for side in sides:
            @pl.when(has(side))
            def _(side=side):
                getattr(make(side), action)()

    def send_margins(r, h):
        each(range(6), functools.partial(margin_copy, r, h), "start")

    def await_margins(r, h):
        each(range(6), functools.partial(margin_arrival, r, h), "wait_recv")

    def tiles(body, rows=own):
        tm = TM if rows == own else TE

        def step(i, carry):
            body(pl.ds(pl.multiple_of(i * tm, tm), tm), pl.ds(i * (tm // BLK), tm // BLK))
            return carry
        lax.fori_loop(0, rows // tm, step, 0)

    loads[0].wait()
    for side in range(6):
        base_l[pl.ds(side * BLK, BLK), :] = phi[picks[side]]
    each(range(6), lambda side: base_copy(side, side ^ 1), "start")
    phi_t = phi[...].reshape(own, ncg).T
    for h in range(HALVES):
        loads[1 + h].wait()
        if h == HALVES - 1:
            loads[4].start()
        part[h] = dot(phi_t, resid[h].reshape(own, width).astype(BF))

    n_line = sizes["gx"]
    low = at["gx"] < n_line // 2

    def pass_on(h, slot):
        @pl.when(has(slot))
        def _():
            line_copy(h, slot, slot).wait_recv()

        @pl.when(has(slot ^ 1))
        def _():
            line_out[slot ^ 1, h] = (line_in[slot, h].astype(F32) + part[h]).astype(BF)
            line_copy(h, slot ^ 1, slot).start()

    def pass_all(slot):
        for h in range(HALVES):
            pass_on(h, slot)

    pl.when(low)(lambda: pass_all(0))
    pl.when(jnp.logical_not(low))(lambda: pass_all(1))

    loads[4].wait()
    loads[5].start()
    for side in range(6):
        k_lent[pl.ds(side * BLK, BLK), :] = kmat[picks[side], :, 0:own]
    each(range(6), lambda side: base_copy(side, side), "wait_recv")

    def weigh(rows, blocks):
        first = dot(flat(kmat[blocks, :, 0:own]), phi[...].reshape(own, ncg))
        first = first + dot(flat(kmat[blocks, :, own:own + 2 * BLK]), base_m[0:2 * BLK, :])
        weights[rows, 0:ncg] = first.astype(BF)
        for side in range(2, 6):
            weights[rows, (side - 1) * ncg:side * ncg] = dot(
                flat(kmat[blocks, :, own + side * BLK:own + (side + 1) * BLK]),
                base_m[side * BLK:(side + 1) * BLK, :]).astype(BF)

    tiles(weigh)

    pl.when(low)(lambda: pass_all(1))
    pl.when(jnp.logical_not(low))(lambda: pass_all(0))

    loads[3].wait()
    for h in range(HALVES):
        total = line_in[0, h].astype(F32) + part[h] + line_in[1, h].astype(F32)
        sols[h, 0:ncg, :] = jnp.dot(
            ecoarse[...], total, precision=lax.Precision.HIGHEST,
            preferred_element_type=F32).astype(BF)
        each(range(2, 6), lambda side, h=h: sol_copy(h, side, side ^ 1), "start")
    for h in range(HALVES):
        def coarse(rows, blocks, h=h):
            acc[h, rows, :] = dot(flat(phi[blocks]), sols[h, 0:ncg, :])
        tiles(coarse)

    def lend_resid(r, h, with_own):
        for side in range(6):
            block = pl.ds(side * BLK, BLK)
            value = resid[h, picks[side]]
            if with_own:
                value = value - e_lent[h, block, :]
            lent[r, h, block, :] = value.astype(BF)
        send_margins(r, h)

    for h in range(HALVES):
        each(range(2, 6), lambda side, h=h: sol_copy(h, side, side), "wait_recv")

        def first_resid(rows, blocks, h=h):
            value = flat(resid[h, blocks]) - dot(weights[rows, :], sols[h])
            resid[h, blocks] = value.reshape(-1, BLK, width)
            resid_b[h, rows, :] = value.astype(BF)
        tiles(first_resid)
        lend_resid(0, h, False)

    loads[5].wait()

    def solve_own(h):
        def body(rows, blocks):
            y[h, rows, :] = dot(ainv[rows, 0:own], resid_b[h])
        tiles(body)

    for h in range(HALVES):
        solve_own(h)

    for c in range(NCOLOR):
        mine = (color == c).astype(F32)
        last = c == NCOLOR - 1
        for h in range(HALVES):
            await_margins(2 * c, h)

            def solve(rows, blocks, h=h):
                value = (y[h, rows, :] + dot(ainv[rows, own:], margin[2 * c, h])) * mine
                if last:
                    for before in range(c):
                        value = value + flat(delta[before, h, blocks]).astype(F32)
                    out_b[h, rows, :] = (acc[h, rows, :] + value).astype(BF)
                else:
                    delta[c, h, blocks] = value.astype(BF).reshape(-1, BLK, width)
            tiles(solve)
            if last:
                pltpu.make_async_copy(
                    out_b.at[h], out.at[0, 0, 0, :, h * width:(h + 1) * width],
                    store_sem.at[h]).start()
            else:
                for side in range(6):
                    lent[2 * c + 1, h, pl.ds(side * BLK, BLK), :] = delta[c, h, picks[side]]
                send_margins(2 * c + 1, h)
        if last:
            break
        for h in range(HALVES):
            def own_part(rows, blocks, h=h):
                value = dot(k_lent[rows, :], delta[c, h].reshape(own, width))
                if c == 0:
                    e_lent[h, rows, :] = value
                else:
                    e_lent[h, rows, :] += value
            tiles(own_part, 6 * BLK)
        for h in range(HALVES):
            await_margins(2 * c + 1, h)

            def update(rows, blocks, h=h):
                value = flat(resid[h, blocks]) - dot(flat(kmat[blocks, :, own:]), margin[2 * c + 1, h])
                resid[h, blocks] = value.reshape(-1, BLK, width)
                resid_b[h, rows, :] = value.astype(BF)
            tiles(update)
            lend_resid(2 * c + 2, h, True)
        for h in range(HALVES):
            solve_own(h)

    for h in range(HALVES):
        pltpu.make_async_copy(
            out_b.at[h], out.at[0, 0, 0, :, h * width:(h + 1) * width], store_sem.at[h]).wait()
    each(range(6), lambda side: base_copy(side, side ^ 1), "wait_send")
    for h in range(HALVES):
        each(range(2), lambda side, h=h: line_copy(h, side, side ^ 1), "wait_send")
        each(range(2, 6), lambda side, h=h: sol_copy(h, side, side ^ 1), "wait_send")
        for r in range(2 * NCOLOR - 1):
            each(range(6), functools.partial(margin_copy, r, h), "wait_send")


def in_blocks(x):
    return x.reshape(x.shape[:-2] + (x.shape[-2] // BLK, BLK, x.shape[-1]))


def body(sizes, rhs, stiff, inv_local, basis, coarse_inv, colors, lend):
    own, nrhs = rhs.shape[-2:]
    sub = stiff.shape[-1]
    ncg = basis.shape[-1]
    width = nrhs // HALVES
    count = own // BLK
    rounds = 2 * NCOLOR - 1
    edge = 6 * BLK
    dma = pltpu.SemaphoreType.DMA
    smem = pl.BlockSpec(memory_space=pltpu.SMEM)
    anyw = pl.BlockSpec(memory_space=pl.ANY)
    result = pl.pallas_call(
        functools.partial(kernel, sizes),
        out_shape=jax.ShapeDtypeStruct(rhs.shape, BF),
        in_specs=[smem, smem] + [anyw] * 5,
        out_specs=anyw,
        scratch_shapes=[
            pltpu.VMEM((count, BLK, sub), BF),
            pltpu.VMEM((own, sub), BF),
            pltpu.VMEM((count, BLK, ncg), BF),
            pltpu.VMEM((ncg, ncg), F32),
            pltpu.VMEM((HALVES, count, BLK, width), F32),
            pltpu.VMEM((HALVES, own, width), BF),
            pltpu.VMEM((HALVES, own, width), F32),
            pltpu.VMEM((NCOLOR - 1, HALVES, count, BLK, width), BF),
            pltpu.VMEM((HALVES, own, width), F32),
            pltpu.VMEM((HALVES, own, width), BF),
            pltpu.VMEM((rounds, HALVES, edge, width), BF),
            pltpu.VMEM((rounds, HALVES, edge, width), BF),
            pltpu.VMEM((edge, own), BF),
            pltpu.VMEM((HALVES, edge, width), F32),
            pltpu.VMEM((own, 5 * ncg), BF),
            pltpu.VMEM((HALVES, 5 * ncg, width), BF),
            pltpu.VMEM((edge, ncg), BF),
            pltpu.VMEM((edge, ncg), BF),
            pltpu.VMEM((HALVES, ncg, width), F32),
            pltpu.VMEM((2, HALVES, ncg, width), BF),
            pltpu.VMEM((2, HALVES, ncg, width), BF),
            dma((6,)),
            dma((HALVES,)),
            dma((rounds, HALVES, 6)),
            dma((rounds, HALVES, 6)),
            dma((HALVES, 6)),
            dma((HALVES, 6)),
            dma((6,)),
            dma((6,)),
            dma((2, HALVES)),
            dma((2, HALVES)),
        ],
        compiler_params=pltpu.CompilerParams(
            collective_id=0, has_side_effects=True, vmem_limit_bytes=58 * 2**20),
    )(colors, lend, in_blocks(rhs), in_blocks(stiff), inv_local, in_blocks(basis), coarse_inv)
    return result.astype(F32)


def solution(mesh):
    in_specs = (
        P("gx", "gy", "col", None, None),
        P("gx", "gy", "col", None, None),
        P("gx", "gy", "col", None, None),
        P("gx", "gy", "col", None, None),
        P("gy", "col", None, None),
        P("gx", "gy", "col"),
        P("gx", "gy", "col", None),
    )
    out_specs = P("gx", "gy", "col", None, None)
    return jax.shard_map(functools.partial(body, dict(mesh.shape)), mesh=mesh,
                         in_specs=in_specs, out_specs=out_specs, check_vma=False)
```
